32 devices in a mesh: comp: 2 (over y), gy: 4 (over z), gx: 4 (over x, core).
Axes of the slice: x: 2, y: 2, z: 4, core: 2. Of those that a mesh axis runs over, the one named last changes fastest.
Arguments:
- spectra: float32 [32, 36, 16, 512], P('comp', None, 'gy', 'gx'), may hold values from 0.05 to 2
- wind_field: float32 [2, 16, 512], P(None, 'gy', 'gx'), may hold values from -5 to 5
- sea_mask: int32 [16, 512], P('gy', 'gx'), may hold values 0 or 1
- first_layer: bfloat16 [1152, 1024], replicated, may hold values from -0.1875 to 0.1875
- second_layer: bfloat16 [1024, 1152], replicated, may hold values from -0.1875 to 0.1875
- ocean_state: float32 [4, 16, 16, 512], P(None, None, 'gy', 'gx'), may hold values from -4 to 4
- current_blocks: float32 [16, 2, 512, 128], P('gy', None, 'gx'), may hold values from 0 to 1
- current_rows: int32 [16, 2, 4], P('gy', None, 'gx'), may hold values from 0 to 15, as said below
- stress_blocks: float32 [16, 2, 512, 128], P('gy', None, 'gx'), may hold values from 0 to 1
- stress_rows: int32 [16, 2, 4], P('gy', None, 'gx'), may hold values from 0 to 15, as said below
Outputs:
- spectra_next: float32 [32, 36, 16, 512], P('comp', None, 'gy', 'gx')
- ocean_next: float32 [4, 16, 16, 512], P(None, None, 'gy', 'gx')
The draws below stay inside these ranges and needn't reach their ends.
Inputs may be any that keep to these rules, and one draw needn't show every extreme that they name: `current_rows`: entry [r, b, t] is the source row read by block b of destination row r in column tile t; it lies within one row of r, and both r - 1 and r + 1 occur. `stress_rows`: entry [r, b, t] is the source row read by block b of destination row r in column tile t; it lies within one row of r, and both r - 1 and r + 1 occur.
All inputs are finite; a program needn't handle non-finite values. No bound on the sum of `sea_mask` on one device may be relied on, other than what follows from the above.
Results may differ from the reference program's by a relative error of at most 0.0023.
Values may be sent and summed in bfloat16 or wider, within the bound.
A program may use at most 64 MiB of HBM per device.

```python
import math
import jax
import jax.numpy as jnp
from jax import lax

FREQS = 32
DIRS = 36
HID = 1024
LEV = 16
STEPS = 2
NB = 2
COLS_DEV = 128
NLAT = 16
NLON = 512
TILES_X = 4
K = 1152


def block_weights(key, salt_value):
    folded = jax.random.fold_in(key, salt_value)
    spread_key = jax.random.fold_in(folded, 1)
    diag_key = jax.random.fold_in(folded, 2)
    spread_part = jax.random.uniform(spread_key, (NLAT, NB, NLON, COLS_DEV), jnp.float32, 0.0, 3.0 / COLS_DEV)
    diag_scale = jax.random.uniform(diag_key, (NLAT, NB, NLON, COLS_DEV), jnp.float32, 0.1, 0.6)
    column_pos = jnp.arange(NLON) % COLS_DEV
    diagonal = (column_pos[:, None] == jnp.arange(COLS_DEV)[None, :]).astype(jnp.float32)
    return diagonal[None, None, :, :] * diag_scale + spread_part


def source_table(key, salt_value):
    folded = jax.random.fold_in(key, salt_value)
    offsets = jax.random.randint(folded, (NLAT, NB, TILES_X), -1, 2)
    row_pos = jnp.arange(NLAT)[:, None, None]
    block_pos = jnp.arange(NB)[None, :, None]
    row_table = jnp.clip(row_pos + offsets, 0, NLAT - 1)
    row_table = jnp.where((row_pos == 0) & (block_pos == 0), 0, row_table)
    row_table = jnp.where((row_pos == NLAT - 1) & (block_pos == 0), NLAT - 1, row_table)
    row_table = jnp.where((row_pos == 1) & (block_pos == 0), 0, row_table)
    row_table = jnp.where((row_pos == NLAT - 2) & (block_pos == 0), NLAT - 1, row_table)
    return row_table.astype(jnp.int32)


def draw_current_blocks(key, part):
    return block_weights(key, 11)


def draw_stress_blocks(key, part):
    return block_weights(key, 23)


def draw_current_rows(key, part):
    return source_table(key, 37)


def draw_stress_rows(key, part):
    return source_table(key, 41)


def place_ends(values, rng, smallest, largest):
    longest = values.shape.index(max(values.shape))
    spots = []
    for shift in (0, 1):
        where = [jax.random.randint(jax.random.fold_in(rng, axis), (), 0, length) for axis, length in enumerate(values.shape)]
        where[longest] = (where[longest] + shift) % values.shape[longest]
        spots.append(tuple(where))
    return values.at[spots[0]].set(smallest).at[spots[1]].set(largest)


def block_scale(rng, dims, cuts, smallest, top_value):
    loudness, own = 1.0, jax.random.fold_in(rng, 6)
    for axis_at, shards_of in cuts:
        steps = jnp.exp(jax.random.uniform(jax.random.fold_in(own, axis_at), (shards_of,), jnp.float32, smallest / len(cuts), top_value / len(cuts)))
        loudness = loudness * jnp.repeat(steps, dims[axis_at] // shards_of).reshape([-1 if axis == axis_at else 1 for axis in range(len(dims))])
    return loudness


def noise(own_key, extent, scale, bound, shards=(), kind=jnp.bfloat16):
    factor_of = block_scale(own_key, extent, shards, -0.22, 0.18) if shards else 1.0
    entries = jax.random.normal(own_key, extent, jnp.float32) * scale * factor_of
    return jnp.minimum(jnp.maximum(entries, -bound), bound).astype(kind)


def setup_inputs(seed: int = 0) -> dict:
    keys = jax.random.split(jax.random.key(seed), 11)
    spectra = jnp.clip(jnp.exp(math.log(2.0) - 3.6888794 * jax.random.uniform(keys[0], (FREQS, DIRS, NLAT, NLON), jnp.float32) ** block_scale(keys[0], (FREQS, DIRS, NLAT, NLON), ((0, 2), (2, 4), (3, 4)), -0.2, 0.2)), 0.05, 2.0)
    wind_field = noise(keys[1], (2, NLAT, NLON), 2.0, 5.0, ((1, 4), (2, 4)), jnp.float32)
    sea_mask = place_ends((jax.random.randint(keys[2], (NLAT, NLON), 0, 10) < 9).astype(jnp.int32), jax.random.fold_in(keys[2], 1), 0, 1)
    first_layer = noise(keys[3], (K, HID), K ** -0.5, 0.1875)
    second_layer = noise(keys[4], (HID, K), HID ** -0.5, 0.1875)
    ocean_state = noise(keys[5], (4, LEV, NLAT, NLON), 1.0, 4.0, ((2, 4), (3, 4)), jnp.float32)
    current_blocks = draw_current_blocks(jax.random.fold_in(keys[10], 71), 0)
    current_rows = draw_current_rows(jax.random.fold_in(keys[10], 71), 0)
    stress_blocks = draw_stress_blocks(jax.random.fold_in(keys[10], 71), 0)
    stress_rows = draw_stress_rows(jax.random.fold_in(keys[10], 71), 0)
    return {"spectra": spectra, "wind_field": wind_field, "sea_mask": sea_mask, "first_layer": first_layer, "second_layer": second_layer, "ocean_state": ocean_state, "current_blocks": current_blocks, "current_rows": current_rows, "stress_blocks": stress_blocks, "stress_rows": stress_rows}


CURRENT_GAIN = 0.08
WIND_GAIN = 0.06
DECAY_GAIN = 0.03
NONLINEAR_GAIN = 0.3
THERMAL = 0.2
HALINE = 0.8
CORIOLIS = 0.1
PRESSURE_GAIN = 0.2
LATERAL_MIX = 0.1
VERTICAL_MIX = 0.2
ADVECTION = 0.3
STRESS_GAIN = 150.0


def spectral_tables(first, count, total, directions):
    freq_index = (jnp.arange(count) + first).astype(jnp.float32)
    group_speed = 0.4 * jnp.exp(-3.0 * freq_index / (total - 1))
    phase_speed = 4.0 * group_speed
    freq_ratio = jnp.exp(2.0 * freq_index / (total - 1) - 1.0)
    angles = 2.0 * jnp.pi * jnp.arange(directions).astype(jnp.float32) / directions
    return group_speed, phase_speed, freq_ratio, jnp.cos(angles), jnp.sin(angles)


def advect(spectrum, padded, group_speed, cosines, sines, currents, mask_f):
    western = padded[:, :, 1:-1, :-2]
    eastern = padded[:, :, 1:-1, 2:]
    southern = padded[:, :, :-2, 1:-1]
    northern = padded[:, :, 2:, 1:-1]
    speed_x = group_speed[:, None, None, None] * cosines[None, :, None, None] + CURRENT_GAIN * currents[0]
    speed_y = group_speed[:, None, None, None] * sines[None, :, None, None] + CURRENT_GAIN * currents[1]
    flux_sum = jnp.maximum(speed_x, 0.0) * (spectrum - western) + jnp.minimum(speed_x, 0.0) * (eastern - spectrum)
    flux_sum = flux_sum + jnp.maximum(speed_y, 0.0) * (spectrum - southern) + jnp.minimum(speed_y, 0.0) * (northern - spectrum)
    return mask_f * (spectrum - flux_sum)


def source_rates(propagated, wind_field, phase_speed, freq_ratio, cosines, sines):
    growth = WIND_GAIN * jnp.maximum(wind_field[0] * cosines[None, :, None, None] + wind_field[1] * sines[None, :, None, None] - phase_speed[:, None, None, None], 0.0)
    energy = jnp.sum(propagated, axis=(0, 1))
    moment = jnp.sum(freq_ratio[:, None, None, None] * propagated, axis=(0, 1))
    push_x = jnp.sum(growth * propagated * cosines[None, :, None, None], axis=(0, 1))
    push_y = jnp.sum(growth * propagated * sines[None, :, None, None], axis=(0, 1))
    return growth, (energy, moment, push_x, push_y)


def contract(left, right):
    return lax.dot_general(left, right, (((0,), (0,)), ((), ())), preferred_element_type=jnp.float32)


def ocean_update(padded, stress, mask_f):
    def middle(field):
        return field[..., 1:-1, 1:-1]

    def eastern(field):
        return field[..., 1:-1, 2:]

    def western(field):
        return field[..., 1:-1, :-2]

    def northern(field):
        return field[..., 2:, 1:-1]

    def southern(field):
        return field[..., :-2, 1:-1]

    def spread(field):
        return eastern(field) + western(field) + northern(field) + southern(field) - 4.0 * middle(field)

    def column(field):
        upper_level = jnp.concatenate([field[:1], field[:-1]], axis=0)
        lower_level = jnp.concatenate([field[1:], field[-1:]], axis=0)
        return upper_level + lower_level - 2.0 * field

    density = -THERMAL * padded[2] + HALINE * padded[3]
    pressure = jnp.cumsum(density, axis=0) - 0.5 * density
    speed_u = middle(padded[0])
    speed_v = middle(padded[1])

    def carry_term(field):
        return speed_u * 0.5 * (eastern(field) - western(field)) + speed_v * 0.5 * (northern(field) - southern(field))

    surface = (jnp.arange(padded.shape[1]) == 0).astype(jnp.float32)[:, None, None]
    tend_u = CORIOLIS * speed_v - PRESSURE_GAIN * 0.5 * (eastern(pressure) - western(pressure)) + LATERAL_MIX * spread(padded[0]) + VERTICAL_MIX * column(speed_u) + STRESS_GAIN * surface * stress[0]
    tend_v = -CORIOLIS * speed_u - PRESSURE_GAIN * 0.5 * (northern(pressure) - southern(pressure)) + LATERAL_MIX * spread(padded[1]) + VERTICAL_MIX * column(speed_v) + STRESS_GAIN * surface * stress[1]
    tend_t = -ADVECTION * carry_term(padded[2]) + LATERAL_MIX * spread(padded[2]) + VERTICAL_MIX * column(middle(padded[2]))
    tend_s = -ADVECTION * carry_term(padded[3]) + LATERAL_MIX * spread(padded[3]) + VERTICAL_MIX * column(middle(padded[3]))
    return middle(padded) + mask_f * jnp.stack([tend_u, tend_v, tend_t, tend_s])


def regrid(field, blocks, row_table):
    tiled = field.reshape(2, NLAT, TILES_X, COLS_DEV).transpose(0, 2, 1, 3)
    tile_index = jnp.arange(TILES_X)[None, None, :]
    selected = tiled[:, tile_index, row_table, :]
    weights = blocks.reshape(NLAT, NB, TILES_X, COLS_DEV, COLS_DEV)
    result = jnp.einsum("rbtds,krbts->krtd", weights, selected, precision=lax.Precision.HIGHEST)
    return result.reshape(2, NLAT, NLON)


def reference(spectra, wind_field, sea_mask, first_layer, second_layer, ocean_state, current_blocks, current_rows, stress_blocks, stress_rows):
    mask_f = sea_mask.astype(jnp.float32)
    currents = regrid(jnp.stack([ocean_state[0, 0], ocean_state[1, 0]]), current_blocks, current_rows)
    group_speed, phase_speed, freq_ratio, cosines, sines = spectral_tables(0, FREQS, FREQS, DIRS)
    spectrum = spectra
    stress_sum = jnp.zeros((2, NLAT, NLON), jnp.float32)

    def network(row_block):
        hidden = jax.nn.silu(contract(first_layer, row_block)).astype(jnp.bfloat16)
        return contract(second_layer, hidden).astype(jnp.bfloat16)

    for step_index in range(STEPS):
        padded = jnp.pad(spectrum, ((0, 0), (0, 0), (1, 1), (1, 1)))
        propagated = advect(spectrum, padded, group_speed, cosines, sines, currents, mask_f)
        growth, partials = source_rates(propagated, wind_field, phase_speed, freq_ratio, cosines, sines)
        energy, moment, push_x, push_y = partials
        energy_floor = jnp.maximum(energy, 1.0)
        scaled = (propagated * (K / energy_floor)).astype(jnp.bfloat16)
        by_rows = jnp.transpose(scaled, (2, 0, 1, 3)).reshape(NLAT, K, NLON)
        transfer = lax.map(network, by_rows).reshape(NLAT, FREQS, DIRS, NLON).transpose(1, 2, 0, 3)
        damping = DECAY_GAIN * freq_ratio[:, None, None, None] * (moment / energy_floor) ** 2
        spectrum = propagated * jnp.exp(growth - damping) + NONLINEAR_GAIN * (energy_floor / K) * transfer.astype(jnp.float32)
        stress_sum = stress_sum + jnp.stack([push_x, push_y]) / K
    stress_ocean = regrid(stress_sum / STEPS, stress_blocks, stress_rows)
    padded_ocean = jnp.pad(ocean_state, ((0, 0), (0, 0), (1, 1), (1, 1)))
    return spectrum, ocean_update(padded_ocean, stress_ocean, mask_f)
```

```python
import numpy as np

import jax
import jax.numpy as jnp
from jax import lax
from jax.experimental import pallas as pl
from jax.experimental.pallas import tpu as pltpu
from jax.sharding import PartitionSpec as P

STEPS = 2


CURRENT_GAIN = 0.08
WIND_GAIN = 0.06
DECAY_GAIN = 0.03
NONLINEAR_GAIN = 0.3
THERMAL = 0.2
HALINE = 0.8
CORIOLIS = 0.1
PRESSURE_GAIN = 0.2
LATERAL_MIX = 0.1
VERTICAL_MIX = 0.2
ADVECTION = 0.3
STRESS_GAIN = 150.0


def from_lower(block, axis):
    count = lax.axis_size(axis)
    return lax.ppermute(block, axis, [(i, i + 1) for i in range(count - 1)])


def from_upper(block, axis):
    count = lax.axis_size(axis)
    return lax.ppermute(block, axis, [(i + 1, i) for i in range(count - 1)])


def partner_of(block):
    return lax.ppermute(block, "comp", [(0, 1), (1, 0)])


def tables(total, directions):
    index = np.arange(total, dtype=np.float64)
    group = 0.4 * np.exp(-3.0 * index / (total - 1))
    ratio = np.exp(2.0 * index / (total - 1) - 1.0)
    angles = 2.0 * np.pi * np.arange(directions) / directions
    cosines, sines = np.cos(angles), np.sin(angles)
    full = np.zeros((total, directions, 8))
    full[..., 0] = group[:, None] * cosines
    full[..., 1] = group[:, None] * sines
    full[..., 2] = cosines
    full[..., 3] = sines
    full[..., 4] = 4.0 * group[:, None]
    full[..., 5] = ratio[:, None]
    return full.reshape(total * directions, 8).astype(np.float32)


VMEM_LIMIT = 56 * 1024 * 1024
CHUNK = 48


def call(kernel, outs, scratch=(), flops=0, moved=0):
    return pl.pallas_call(
        kernel,
        out_shape=outs,
        scratch_shapes=list(scratch),
        compiler_params=pltpu.CompilerParams(vmem_limit_bytes=VMEM_LIMIT),
        cost_estimate=pl.CostEstimate(flops=flops, bytes_accessed=moved, transcendentals=0),
    )


def edges_kernel(state, low, high, ends):
    rows = state.shape[1]
    low[...] = state[:, 0, :].astype(jnp.bfloat16)
    high[...] = state[:, rows - 1, :].astype(jnp.bfloat16)
    for r in range(rows):
        values = state[:, r, :]
        ends[:, r : r + 1] = values[:, :1]
        ends[:, rows + r : rows + r + 1] = values[:, -1:]


def advect_kernel(state, south, north, west, east, table, currents, wind, mask, prop, prop_16, sums):
    comps, rows, cols = state.shape
    lane = lax.broadcasted_iota(jnp.int32, (CHUNK, cols), 1)

    def body(i, totals):
        part = pl.ds(pl.multiple_of(i * CHUNK, CHUNK), CHUNK)
        tab = table[part, :]
        gx, gy, cos, sin, phase, ratio = (
            jnp.broadcast_to(tab[:, n : n + 1], (CHUNK, cols)) for n in range(6)
        )
        near_w = west[part, :]
        near_e = east[part, :]
        lines = [south[part, :].astype(jnp.float32)]
        lines += [state[part, r, :] for r in range(rows)]
        lines += [north[part, :].astype(jnp.float32)]
        out = []
        for r in range(rows):
            here = lines[r + 1]
            before = jnp.where(lane == 0, near_w[:, r : r + 1], pltpu.roll(here, 1, 1))
            after = jnp.where(lane == cols - 1, near_e[:, r : r + 1], pltpu.roll(here, cols - 1, 1))
            cx = gx + CURRENT_GAIN * currents[0, r : r + 1, :]
            cy = gy + CURRENT_GAIN * currents[1, r : r + 1, :]
            flux = jnp.abs(cx) * (here - jnp.where(cx > 0.0, before, after))
            flux = flux + jnp.abs(cy) * (here - jnp.where(cy > 0.0, lines[r], lines[r + 2]))
            moved = mask[r : r + 1, :] * (here - flux)
            prop[r, part, :] = moved
            prop_16[part, r * cols : (r + 1) * cols] = moved.astype(jnp.bfloat16)
            growth = WIND_GAIN * jnp.maximum(
                wind[0, r : r + 1, :] * cos + wind[1, r : r + 1, :] * sin - phase, 0.0
            )
            pushed = growth * moved
            for value in (moved, ratio * moved, pushed * cos, pushed * sin):
                out.append(value.reshape(CHUNK // 8, 8, cols).sum(axis=0))
        return tuple(t + o for t, o in zip(totals, out))

    zero = jnp.zeros((8, cols), jnp.float32)
    totals = lax.fori_loop(0, comps // CHUNK, body, (zero,) * (4 * rows))
    for r in range(rows):
        for n in range(4):
            sums[n * rows + r : n * rows + r + 1, :] = totals[4 * r + n].sum(axis=0, keepdims=True)


def dot_0(left, right):
    return lax.dot_general(
        left, right, (((0,), (0,)), ((), ())), preferred_element_type=jnp.float32
    )


def own_kernel(first, prop_16, partial):
    comps = prop_16.shape[0]
    start = pl.multiple_of(lax.axis_index("comp") * comps, comps)
    partial[...] = dot_0(first[pl.ds(start, comps), :], prop_16[...])


def update_kernel(
    first, second, other_16, partial, prop, sums, other_sums, table, wind,
    state, low, high, ends, hidden, transfer,
):
    rows, comps, cols = prop.shape
    start = pl.multiple_of((1 - lax.axis_index("comp")) * comps, comps)
    scale_up = 2.0 * comps
    total = sums[...] + other_sums[...]
    floor = jnp.maximum(total[:rows, :], 1.0)
    spread_ratio = total[rows : 2 * rows, :] / floor
    squared = DECAY_GAIN * spread_ratio * spread_ratio
    gain = scale_up / floor
    back = NONLINEAR_GAIN * (floor / scale_up)
    pre = dot_0(first[pl.ds(start, comps), :], other_16[...]) + partial[...]
    pre = pre * jnp.concatenate([gain[r : r + 1, :] for r in range(rows)], axis=1)
    hidden[...] = (pre / (1.0 + jnp.exp(-pre))).astype(jnp.bfloat16)
    transfer[...] = dot_0(second[...], hidden[...]).astype(jnp.bfloat16)

    def body(i, carry):
        part = pl.ds(pl.multiple_of(i * CHUNK, CHUNK), CHUNK)
        tab = table[part, :]
        cos, sin, phase, ratio = (
            jnp.broadcast_to(tab[:, n : n + 1], (CHUNK, cols)) for n in range(2, 6)
        )
        for r in range(rows):
            growth = WIND_GAIN * jnp.maximum(
                wind[0, r : r + 1, :] * cos + wind[1, r : r + 1, :] * sin - phase, 0.0
            )
            fresh = prop[r, part, :] * jnp.exp(growth - ratio * squared[r : r + 1, :])
            fresh = fresh + back[r : r + 1, :] * transfer[part, r * cols : (r + 1) * cols].astype(
                jnp.float32
            )
            state[part, r, :] = fresh
            ends[part, r : r + 1] = fresh[:, :1]
            ends[part, rows + r : rows + r + 1] = fresh[:, cols - 1 :]
            if r == 0:
                low[part, :] = fresh.astype(jnp.bfloat16)
            if r == rows - 1:
                high[part, :] = fresh.astype(jnp.bfloat16)
        return carry

    lax.fori_loop(0, comps // CHUNK, body, 0)


def ocean_update(padded, stress, mask_f):

    def middle(field):
        return field[..., 1:-1, 1:-1]

    def eastern(field):
        return field[..., 1:-1, 2:]

    def western(field):
        return field[..., 1:-1, :-2]

    def northern(field):
        return field[..., 2:, 1:-1]

    def southern(field):
        return field[..., :-2, 1:-1]

    def spread(field):
        return (
            eastern(field)
            + western(field)
            + northern(field)
            + southern(field)
            - 4.0 * middle(field)
        )

    def column(field):
        upper_level = jnp.concatenate([field[:1], field[:-1]], axis=0)
        lower_level = jnp.concatenate([field[1:], field[-1:]], axis=0)
        return upper_level + lower_level - 2.0 * field

    density = -THERMAL * padded[2] + HALINE * padded[3]
    pressure = jnp.cumsum(density, axis=0) - 0.5 * density
    speed_u = middle(padded[0])
    speed_v = middle(padded[1])

    def carry_term(field):
        return speed_u * 0.5 * (eastern(field) - western(field)) + speed_v * 0.5 * (
            northern(field) - southern(field)
        )

    surface = (jnp.arange(padded.shape[1]) == 0).astype(jnp.float32)[:, None, None]
    tend_u = (
        CORIOLIS * speed_v
        - PRESSURE_GAIN * 0.5 * (eastern(pressure) - western(pressure))
        + LATERAL_MIX * spread(padded[0])
        + VERTICAL_MIX * column(speed_u)
        + STRESS_GAIN * surface * stress[0]
    )
    tend_v = (
        -CORIOLIS * speed_u
        - PRESSURE_GAIN * 0.5 * (northern(pressure) - southern(pressure))
        + LATERAL_MIX * spread(padded[1])
        + VERTICAL_MIX * column(speed_v)
        + STRESS_GAIN * surface * stress[1]
    )
    tend_t = (
        -ADVECTION * carry_term(padded[2])
        + LATERAL_MIX * spread(padded[2])
        + VERTICAL_MIX * column(middle(padded[2]))
    )
    tend_s = (
        -ADVECTION * carry_term(padded[3])
        + LATERAL_MIX * spread(padded[3])
        + VERTICAL_MIX * column(middle(padded[3]))
    )
    return middle(padded) + mask_f * jnp.stack([tend_u, tend_v, tend_t, tend_s])


def regrid(field, below, above, blocks, row_table):
    rows = field.shape[1]
    padded = jnp.concatenate([below, field, above], axis=1)
    first_row = lax.axis_index("gy") * rows
    offset = row_table[:, :, 0] - first_row - jnp.arange(rows)[:, None]
    offset = offset[None, :, :, None]
    selected = jnp.where(
        offset < 0,
        padded[:, :rows, None, :],
        jnp.where(offset == 0, padded[:, 1:-1, None, :], padded[:, 2:, None, :]),
    )
    return jnp.einsum("rbds,krbs->krd", blocks, selected, precision=lax.Precision.HIGHEST)


def local(
    spectra,
    wind_field,
    sea_mask,
    first_layer,
    second_layer,
    ocean_state,
    current_blocks,
    current_rows,
    stress_blocks,
    stress_rows,
):
    f32, b16 = jnp.float32, jnp.bfloat16
    mask_f = sea_mask.astype(f32)
    rows, cols = sea_mask.shape
    half_freqs, directions = spectra.shape[:2]
    comps = half_freqs * directions
    total = 2 * comps
    units = first_layer.shape[1]
    cells = rows * cols
    me = lax.axis_index("comp")
    table = lax.dynamic_slice_in_dim(
        jnp.asarray(tables(2 * half_freqs, directions)), me * comps, comps, 0
    )
    shape = jax.ShapeDtypeStruct
    edge_outs = (shape((comps, cols), b16), shape((comps, cols), b16), shape((comps, 2 * rows), f32))
    state = spectra.reshape(comps, rows, cols)
    low, high, ends = call(edges_kernel, edge_outs, moved=3 * comps * cells)(state)
    ocean_low, ocean_high = ocean_state[:, :, :1], ocean_state[:, :, -1:]
    ocean_south = from_lower(ocean_high, "gy")
    ocean_north = from_upper(ocean_low, "gy")
    ocean_west = from_lower(ocean_state[..., -1], "gx")[..., None]
    ocean_east = from_upper(ocean_state[..., 0], "gx")[..., None]
    currents = regrid(
        ocean_state[:2, 0], ocean_south[:2, 0], ocean_north[:2, 0], current_blocks, current_rows
    )
    second_own = lax.dynamic_slice_in_dim(second_layer, me * comps, comps, 1)
    pushes = jnp.zeros((2 * rows, cols), f32)
    for step in range(STEPS):
        south = from_lower(high, "gy")
        north = from_upper(low, "gy")
        flipped = ends.T
        west = from_lower(flipped[rows:], "gx").T
        east = from_upper(flipped[:rows], "gx").T
        prop, prop_16, sums = call(
            advect_kernel,
            (shape((rows, comps, cols), f32), shape((comps, cells), b16), shape((4 * rows, cols), f32)),
            flops=40 * comps * cells,
            moved=12 * comps * cells,
        )(state, south, north, west, east, table, currents, wind_field, mask_f)
        other_sums = partner_of(sums)
        other_16 = partner_of(prop_16)
        partial = call(
            own_kernel,
            shape((units, cells), f32),
            flops=2 * comps * units * cells,
            moved=4 * units * cells + 4 * comps * units,
        )(first_layer, prop_16)
        state, low, high, ends = call(
            update_kernel,
            (shape((comps, rows, cols), f32),) + edge_outs,
            scratch=(pltpu.VMEM((units, cells), b16), pltpu.VMEM((comps, cells), b16)),
            flops=4 * comps * units * cells,
            moved=16 * comps * cells,
        )(first_layer, second_own, other_16, partial, prop, sums, other_sums, table, wind_field)
        pushes = pushes + sums[2 * rows :] + other_sums[2 * rows :]
    stress = (pushes / (STEPS * total)).reshape(2, rows, cols)
    stress_ocean = regrid(
        stress,
        from_lower(stress[:, -1:], "gy"),
        from_upper(stress[:, :1], "gy"),
        stress_blocks,
        stress_rows,
    )
    corner = jnp.zeros(ocean_west.shape[:2] + (1, 1), f32)
    padded = jnp.concatenate(
        [
            jnp.concatenate([corner, ocean_south, corner], axis=3),
            jnp.concatenate([ocean_west, ocean_state, ocean_east], axis=3),
            jnp.concatenate([corner, ocean_north, corner], axis=3),
        ],
        axis=2,
    )
    return (state.reshape(spectra.shape), ocean_update(padded, stress_ocean, mask_f))


def solution(mesh):
    placed = (
        P("comp", None, "gy", "gx"),
        P(None, "gy", "gx"),
        P("gy", "gx"),
        P(),
        P(),
        P(None, None, "gy", "gx"),
        P("gy", None, "gx", None),
        P("gy", None, "gx"),
        P("gy", None, "gx", None),
        P("gy", None, "gx"),
    )
    return jax.shard_map(
        local,
        mesh=mesh,
        in_specs=placed,
        out_specs=(P("comp", None, "gy", "gx"), P(None, None, "gy", "gx")),
        check_vma=False,
    )
```

```python
import numpy as np

import jax
import jax.numpy as jnp
from jax import lax
from jax.experimental import pallas as pl
from jax.experimental.pallas import tpu as pltpu
from jax.sharding import PartitionSpec as P

STEPS = 2


CURRENT_GAIN = 0.08
WIND_GAIN = 0.06
DECAY_GAIN = 0.03
NONLINEAR_GAIN = 0.3
THERMAL = 0.2
HALINE = 0.8
CORIOLIS = 0.1
PRESSURE_GAIN = 0.2
LATERAL_MIX = 0.1
VERTICAL_MIX = 0.2
ADVECTION = 0.3
STRESS_GAIN = 150.0


def from_lower(block, axis):
    count = lax.axis_size(axis)
    return lax.ppermute(block, axis, [(i, i + 1) for i in range(count - 1)])


def from_upper(block, axis):
    count = lax.axis_size(axis)
    return lax.ppermute(block, axis, [(i + 1, i) for i in range(count - 1)])


def tables(total, directions):
    index = np.arange(total, dtype=np.float64)
    group = 0.4 * np.exp(-3.0 * index / (total - 1))
    ratio = np.exp(2.0 * index / (total - 1) - 1.0)
    angles = 2.0 * np.pi * np.arange(directions) / directions
    cosines, sines = np.cos(angles), np.sin(angles)
    full = np.zeros((total, directions, 8))
    full[..., 0] = group[:, None] * cosines
    full[..., 1] = group[:, None] * sines
    full[..., 2] = cosines
    full[..., 3] = sines
    full[..., 4] = 4.0 * group[:, None]
    full[..., 5] = ratio[:, None]
    return full.reshape(total * directions, 8).astype(np.float32)


VMEM_LIMIT = 56 * 1024 * 1024
CHUNK = 48


def dot_0(left, right):
    return lax.dot_general(
        left, right, (((0,), (0,)), ((), ())), preferred_element_type=jnp.float32
    )


def step_kernel(
    first, spectra, second, table, currents, wind, mask,
    state, pushes, push_from,
    prop, prop_16, other_16, ends, ends_t, beside, rows_out, rows_in, sums, other_sums,
    push_out, push_in, hidden, transfer, partial, side_send, side_recv, chunk_send, chunk_recv,
    sum_send, sum_recv, push_send, push_recv,
):
    comps, rows, cols = state.shape
    f32, b16 = jnp.float32, jnp.bfloat16
    chunks = comps // CHUNK
    me = lax.axis_index("comp")
    places = []
    for axis in ("gy", "gx"):
        at, count = lax.axis_index(axis), lax.axis_size(axis)
        places.append((axis, lax.rem(at + 1, count), at < count - 1))
        places.append((axis, lax.rem(at + count - 1, count), at > 0))
    beside[...] = jnp.zeros_like(beside)
    rows_in[...] = jnp.zeros_like(rows_in)
    push_in[...] = jnp.zeros_like(push_in)
    pushes[...] = jnp.zeros_like(pushes)
    ends[...] = jnp.zeros_like(ends)

    mesh_ids = pl.DeviceIdType.MESH
    barrier = pltpu.get_barrier_semaphore()
    for axis, place, there in places:
        @pl.when(there)
        def _(axis=axis, place=place):
            pl.semaphore_signal(barrier, inc=1, device_id={axis: place}, device_id_type=mesh_ids)
    pl.semaphore_signal(barrier, inc=1, device_id={"comp": 1 - me}, device_id_type=mesh_ids)

    def fill(i, carry):
        part = pl.ds(pl.multiple_of(i * CHUNK, CHUNK), CHUNK)
        for r in range(rows):
            line = spectra[part, r, :]
            state[part, r, :] = line
            ends[part, r : r + 1] = line[:, :1]
            ends[part, rows + r : rows + r + 1] = line[:, cols - 1 :]
            if r == 0:
                rows_out[0, 1, part, :] = line.astype(b16)
            if r == rows - 1:
                rows_out[0, 0, part, :] = line.astype(b16)
        return carry

    lax.fori_loop(0, chunks, fill, 0)
    pl.semaphore_wait(barrier, 1 + sum(jnp.where(there, 1, 0) for _, _, there in places))

    def remote(source, target, send, recv, where):
        return pltpu.make_async_remote_copy(
            src_ref=source, dst_ref=target, send_sem=send, recv_sem=recv,
            device_id=where, device_id_type=mesh_ids,
        )

    def side(s, n):
        axis, place, _ = places[n]
        if n < 2:
            source, target = rows_out.at[s, n], rows_in.at[s, n]
        else:
            source, target = ends_t.at[s, pl.ds(0, 8)], beside.at[s, n - 2, pl.ds(0, 8)]
        return remote(source, target, side_send.at[s, n], side_recv.at[s, n], {axis: place})

    def chunk(s, i):
        part = pl.ds(pl.multiple_of(i * CHUNK, CHUNK), CHUNK)
        return remote(
            prop_16.at[s, part], other_16.at[s, part],
            chunk_send.at[s, i], chunk_recv.at[s, i], {"comp": 1 - me},
        )

    def sum_copy(s):
        return remote(sums.at[s], other_sums.at[s], sum_send.at[s], sum_recv.at[s], {"comp": 1 - me})

    def push(n):
        axis, place, _ = places[n]
        return remote(push_out, push_in.at[n], push_send.at[n], push_recv.at[n], {axis: place})

    lane = lax.broadcasted_iota(jnp.int32, (CHUNK, cols), 1)

    def step(s, carry):
        ends_t[s] = ends[...].T
        for n in range(4):
            @pl.when(places[n][2])
            def _(n=n):
                side(s, n).start()
        for n in range(4):
            @pl.when(places[n ^ 1][2])
            def _(n=n):
                side(s, n).wait_recv()
        ends[...] = beside[s, 0].T
        partial[: ends.shape[0], :cols] = beside[s, 1].T

        def body(i, totals):
            part = pl.ds(pl.multiple_of(i * CHUNK, CHUNK), CHUNK)
            tab = table[part, :]
            gx, gy, cos, sin, phase, ratio = (
                jnp.broadcast_to(tab[:, n : n + 1], (CHUNK, cols)) for n in range(6)
            )
            near_w = ends[part, :]
            near_e = partial[part, :cols]
            lines = [rows_in[s, 0, part, :].astype(f32)]
            lines += [state[part, r, :] for r in range(rows)]
            lines += [rows_in[s, 1, part, :].astype(f32)]
            out = []
            for r in range(rows):
                here = lines[r + 1]
                before = jnp.where(
                    lane == 0, near_w[:, rows + r : rows + r + 1], pltpu.roll(here, 1, 1)
                )
                after = jnp.where(
                    lane == cols - 1, near_e[:, r : r + 1], pltpu.roll(here, cols - 1, 1)
                )
                cx = gx + CURRENT_GAIN * currents[0, r : r + 1, :]
                cy = gy + CURRENT_GAIN * currents[1, r : r + 1, :]
                flux = jnp.abs(cx) * (here - jnp.where(cx > 0.0, before, after))
                flux = flux + jnp.abs(cy) * (here - jnp.where(cy > 0.0, lines[r], lines[r + 2]))
                moved = mask[r : r + 1, :] * (here - flux)
                prop[r, part, :] = moved
                prop_16[s, part, r * cols : (r + 1) * cols] = moved.astype(b16)
                growth = WIND_GAIN * jnp.maximum(
                    wind[0, r : r + 1, :] * cos + wind[1, r : r + 1, :] * sin - phase, 0.0
                )
                pushed = growth * moved
                for value in (moved, ratio * moved, pushed * cos, pushed * sin):
                    out.append(value.reshape(CHUNK // 8, 8, cols).sum(axis=0))
            chunk(s, i).start()
            return tuple(t + o for t, o in zip(totals, out))

        zero = jnp.zeros((8, cols), f32)
        totals = lax.fori_loop(0, chunks, body, (zero,) * (4 * rows))
        for r in range(rows):
            for n in range(4):
                at = n * rows + r
                sums[s, at : at + 1, :] = totals[4 * r + n].sum(axis=0, keepdims=True)
        sum_copy(s).start()
        own = pl.multiple_of(me * comps, comps)
        partial[...] = dot_0(first[pl.ds(own, comps), :], prop_16[s])
        sum_copy(s).wait_recv()
        total = sums[s] + other_sums[s]
        pushes[...] += total[2 * rows :, :]

        @pl.when(s == STEPS - 1)
        def _():
            push_out[...] = pushes[...]
            for n in range(2):
                @pl.when(places[n][2])
                def _(n=n):
                    push(n).start()

        scale_up = 2.0 * comps
        floor = jnp.maximum(total[:rows, :], 1.0)
        spread_ratio = total[rows : 2 * rows, :] / floor
        squared = DECAY_GAIN * spread_ratio * spread_ratio
        gain = scale_up / floor
        back = NONLINEAR_GAIN * (floor / scale_up)

        def arrive(i, carry):
            chunk(s, i).wait_recv()
            return carry

        lax.fori_loop(0, chunks, arrive, 0)
        far_start = pl.multiple_of((1 - me) * comps, comps)
        pre = dot_0(first[pl.ds(far_start, comps), :], other_16[s]) + partial[...]
        pre = pre * jnp.concatenate([gain[r : r + 1, :] for r in range(rows)], axis=1)
        hidden[...] = (pre / (1.0 + jnp.exp(-pre))).astype(b16)
        transfer[...] = dot_0(second[...], hidden[...]).astype(b16)
        later = jnp.minimum(s + 1, STEPS - 1)

        for n in range(4):
            @pl.when(places[n][2])
            def _(n=n):
                side(s, n).wait_send()

        def update(i, carry):
            part = pl.ds(pl.multiple_of(i * CHUNK, CHUNK), CHUNK)
            tab = table[part, :]
            cos, sin, phase, ratio = (
                jnp.broadcast_to(tab[:, n : n + 1], (CHUNK, cols)) for n in range(2, 6)
            )
            for r in range(rows):
                growth = WIND_GAIN * jnp.maximum(
                    wind[0, r : r + 1, :] * cos + wind[1, r : r + 1, :] * sin - phase, 0.0
                )
                fresh = prop[r, part, :] * jnp.exp(growth - ratio * squared[r : r + 1, :])
                moved = transfer[part, r * cols : (r + 1) * cols].astype(f32)
                fresh = fresh + back[r : r + 1, :] * moved
                state[part, r, :] = fresh
                ends[part, r : r + 1] = fresh[:, :1]
                ends[part, rows + r : rows + r + 1] = fresh[:, cols - 1 :]
                if r == 0:
                    rows_out[later, 1, part, :] = fresh.astype(b16)
                if r == rows - 1:
                    rows_out[later, 0, part, :] = fresh.astype(b16)
            return carry

        lax.fori_loop(0, chunks, update, 0)

        def leave(i, carry):
            chunk(s, i).wait_send()
            return carry

        lax.fori_loop(0, chunks, leave, 0)
        sum_copy(s).wait_send()
        return carry

    lax.fori_loop(0, STEPS, step, 0)
    for n in range(2):
        @pl.when(places[n][2])
        def _(n=n):
            push(n).wait_send()

        @pl.when(places[n ^ 1][2])
        def _(n=n):
            push(n).wait_recv()
    push_from[...] = push_in[...]


def steps_call(first, state, second, table, currents, wind, mask):
    comps, rows, cols = state.shape
    units = first.shape[1]
    cells = rows * cols
    f32, b16 = jnp.float32, jnp.bfloat16
    wide = -(-comps // 128) * 128
    shape = jax.ShapeDtypeStruct
    dma = pltpu.SemaphoreType.DMA
    chunks = comps // CHUNK
    return pl.pallas_call(
        step_kernel,
        out_shape=(
            shape((comps, rows, cols), f32),
            shape((2 * rows, cols), f32),
            shape((2, 2 * rows, cols), f32),
        ),
        in_specs=[pl.BlockSpec(memory_space=pltpu.VMEM)] * 7,
        out_specs=(pl.BlockSpec(memory_space=pltpu.VMEM),) * 3,
        scratch_shapes=[
            pltpu.VMEM((rows, comps, cols), f32),
            pltpu.VMEM((STEPS, comps, cells), b16),
            pltpu.VMEM((STEPS, comps, cells), b16),
            pltpu.VMEM((wide, 128), f32),
            pltpu.VMEM((STEPS, 128, wide), f32),
            pltpu.VMEM((STEPS, 2, 128, wide), f32),
            pltpu.VMEM((STEPS, 2, comps, cols), b16),
            pltpu.VMEM((STEPS, 2, comps, cols), b16),
            pltpu.VMEM((STEPS, 4 * rows, cols), f32),
            pltpu.VMEM((STEPS, 4 * rows, cols), f32),
            pltpu.VMEM((2 * rows, cols), f32),
            pltpu.VMEM((2, 2 * rows, cols), f32),
            pltpu.VMEM((units, cells), b16),
            pltpu.VMEM((comps, cells), b16),
            pltpu.VMEM((units, cells), f32),
            dma((STEPS, 4)),
            dma((STEPS, 4)),
            dma((STEPS, chunks)),
            dma((STEPS, chunks)),
            dma((STEPS,)),
            dma((STEPS,)),
            dma((2,)),
            dma((2,)),
        ],
        compiler_params=pltpu.CompilerParams(
            vmem_limit_bytes=VMEM_LIMIT, collective_id=0, has_side_effects=True
        ),
        cost_estimate=pl.CostEstimate(
            flops=12 * comps * units * cells, bytes_accessed=24 * comps * cells, transcendentals=0
        ),
    )(first, state, second, table, currents, wind, mask)


def ocean_update(padded, stress, mask_f):

    def middle(field):
        return field[..., 1:-1, 1:-1]

    def eastern(field):
        return field[..., 1:-1, 2:]

    def western(field):
        return field[..., 1:-1, :-2]

    def northern(field):
        return field[..., 2:, 1:-1]

    def southern(field):
        return field[..., :-2, 1:-1]

    def spread(field):
        return (
            eastern(field)
            + western(field)
            + northern(field)
            + southern(field)
            - 4.0 * middle(field)
        )

    def column(field):
        upper_level = jnp.concatenate([field[:1], field[:-1]], axis=0)
        lower_level = jnp.concatenate([field[1:], field[-1:]], axis=0)
        return upper_level + lower_level - 2.0 * field

    density = -THERMAL * padded[2] + HALINE * padded[3]
    pressure = jnp.cumsum(density, axis=0) - 0.5 * density
    speed_u = middle(padded[0])
    speed_v = middle(padded[1])

    def carry_term(field):
        return speed_u * 0.5 * (eastern(field) - western(field)) + speed_v * 0.5 * (
            northern(field) - southern(field)
        )

    surface = (jnp.arange(padded.shape[1]) == 0).astype(jnp.float32)[:, None, None]
    tend_u = (
        CORIOLIS * speed_v
        - PRESSURE_GAIN * 0.5 * (eastern(pressure) - western(pressure))
        + LATERAL_MIX * spread(padded[0])
        + VERTICAL_MIX * column(speed_u)
        + STRESS_GAIN * surface * stress[0]
    )
    tend_v = (
        -CORIOLIS * speed_u
        - PRESSURE_GAIN * 0.5 * (northern(pressure) - southern(pressure))
        + LATERAL_MIX * spread(padded[1])
        + VERTICAL_MIX * column(speed_v)
        + STRESS_GAIN * surface * stress[1]
    )
    tend_t = (
        -ADVECTION * carry_term(padded[2])
        + LATERAL_MIX * spread(padded[2])
        + VERTICAL_MIX * column(middle(padded[2]))
    )
    tend_s = (
        -ADVECTION * carry_term(padded[3])
        + LATERAL_MIX * spread(padded[3])
        + VERTICAL_MIX * column(middle(padded[3]))
    )
    return middle(padded) + mask_f * jnp.stack([tend_u, tend_v, tend_t, tend_s])


def regrid(field, below, above, blocks, row_table):
    rows = field.shape[1]
    padded = jnp.concatenate([below, field, above], axis=1)
    first_row = lax.axis_index("gy") * rows
    offset = row_table[:, :, 0] - first_row - jnp.arange(rows)[:, None]
    offset = offset[None, :, :, None]
    selected = jnp.where(
        offset < 0,
        padded[:, :rows, None, :],
        jnp.where(offset == 0, padded[:, 1:-1, None, :], padded[:, 2:, None, :]),
    )
    return jnp.einsum("rbds,krbs->krd", blocks, selected, precision=lax.Precision.HIGHEST)


def local(
    spectra,
    wind_field,
    sea_mask,
    first_layer,
    second_layer,
    ocean_state,
    current_blocks,
    current_rows,
    stress_blocks,
    stress_rows,
):
    f32 = jnp.float32
    mask_f = sea_mask.astype(f32)
    rows, cols = sea_mask.shape
    half_freqs, directions = spectra.shape[:2]
    comps = half_freqs * directions
    total = 2 * comps
    me = lax.axis_index("comp")
    table = lax.dynamic_slice_in_dim(
        jnp.asarray(tables(2 * half_freqs, directions)), me * comps, comps, 0
    )
    ocean_low, ocean_high = ocean_state[:, :, :1], ocean_state[:, :, -1:]
    ocean_south = from_lower(ocean_high, "gy")
    ocean_north = from_upper(ocean_low, "gy")
    ocean_west = from_lower(ocean_state[..., -1], "gx")[..., None]
    ocean_east = from_upper(ocean_state[..., 0], "gx")[..., None]
    currents = regrid(
        ocean_state[:2, 0], ocean_south[:2, 0], ocean_north[:2, 0], current_blocks, current_rows
    )
    second_own = lax.dynamic_slice_in_dim(second_layer, me * comps, comps, 1)
    state, pushes, push_from = steps_call(
        first_layer,
        spectra.reshape(comps, rows, cols),
        second_own,
        table,
        currents,
        wind_field,
        mask_f,
    )
    whole = jnp.concatenate([pushes[None], push_from]) / (STEPS * total)
    whole = whole.reshape(3, 2, rows, cols)
    stress_ocean = regrid(
        whole[0], whole[1, :, -1:], whole[2, :, :1], stress_blocks, stress_rows
    )
    corner = jnp.zeros(ocean_west.shape[:2] + (1, 1), f32)
    padded = jnp.concatenate(
        [
            jnp.concatenate([corner, ocean_south, corner], axis=3),
            jnp.concatenate([ocean_west, ocean_state, ocean_east], axis=3),
            jnp.concatenate([corner, ocean_north, corner], axis=3),
        ],
        axis=2,
    )
    return (state.reshape(spectra.shape), ocean_update(padded, stress_ocean, mask_f))


def solution(mesh):
    placed = (
        P("comp", None, "gy", "gx"),
        P(None, "gy", "gx"),
        P("gy", "gx"),
        P(),
        P(),
        P(None, None, "gy", "gx"),
        P("gy", None, "gx", None),
        P("gy", None, "gx"),
        P("gy", None, "gx", None),
        P("gy", None, "gx"),
    )
    return jax.shard_map(
        local,
        mesh=mesh,
        in_specs=placed,
        out_specs=(P("comp", None, "gy", "gx"), P(None, None, "gy", "gx")),
        check_vma=False,
    )
```

```python
import numpy as np

import jax
import jax.numpy as jnp
from jax import lax
from jax.experimental import pallas as pl
from jax.experimental.pallas import tpu as pltpu
from jax.sharding import PartitionSpec as P

STEPS = 2


CURRENT_GAIN = 0.08
WIND_GAIN = 0.06
DECAY_GAIN = 0.03
NONLINEAR_GAIN = 0.3
THERMAL = 0.2
HALINE = 0.8
CORIOLIS = 0.1
PRESSURE_GAIN = 0.2
LATERAL_MIX = 0.1
VERTICAL_MIX = 0.2
ADVECTION = 0.3
STRESS_GAIN = 150.0


def tables(total, directions):
    index = np.arange(total, dtype=np.float64)
    group = 0.4 * np.exp(-3.0 * index / (total - 1))
    ratio = np.exp(2.0 * index / (total - 1) - 1.0)
    angles = 2.0 * np.pi * np.arange(directions) / directions
    cosines, sines = np.cos(angles), np.sin(angles)
    full = np.zeros((total, directions, 8))
    full[..., 0] = group[:, None] * cosines
    full[..., 1] = group[:, None] * sines
    full[..., 2] = cosines
    full[..., 3] = sines
    full[..., 4] = 4.0 * group[:, None]
    full[..., 5] = ratio[:, None]
    return full.reshape(total * directions, 8).astype(np.float32)


VMEM_LIMIT = 56 * 1024 * 1024
CHUNK = 48
PIECES = 3


def dot_0(left, right):
    return lax.dot_general(
        left, right, (((0,), (0,)), ((), ())), preferred_element_type=jnp.float32
    )


def step_kernel(
    first, spectra, second, table, currents, wind, mask,
    state, pushes, push_from,
    prop, prop_16, other_16, ends, ends_t, beside, rows_out, rows_in, sums, other_sums,
    push_out, push_in, hidden, transfer, partial, side_send, side_recv, chunk_send, chunk_recv,
    sum_send, sum_recv, push_send, push_recv,
):
    comps, rows, cols = state.shape
    f32, b16 = jnp.float32, jnp.bfloat16
    chunks = comps // CHUNK
    me = lax.axis_index("comp")
    places = []
    for axis in ("gy", "gx"):
        at, count = lax.axis_index(axis), lax.axis_size(axis)
        places.append((axis, lax.rem(at + 1, count), at < count - 1))
        places.append((axis, lax.rem(at + count - 1, count), at > 0))
    beside[...] = jnp.zeros_like(beside)
    rows_in[...] = jnp.zeros_like(rows_in)
    push_in[...] = jnp.zeros_like(push_in)
    pushes[...] = jnp.zeros_like(pushes)
    ends[...] = jnp.zeros_like(ends)

    mesh_ids = pl.DeviceIdType.MESH
    barrier = pltpu.get_barrier_semaphore()
    for axis, place, there in places:
        @pl.when(there)
        def _(axis=axis, place=place):
            pl.semaphore_signal(barrier, inc=1, device_id={axis: place}, device_id_type=mesh_ids)
    pl.semaphore_signal(barrier, inc=1, device_id={"comp": 1 - me}, device_id_type=mesh_ids)

    def fill(i, carry):
        part = pl.ds(pl.multiple_of(i * CHUNK, CHUNK), CHUNK)
        for r in range(rows):
            line = spectra[part, r, :]
            state[part, r, :] = line
            ends[part, r : r + 1] = line[:, :1]
            ends[part, rows + r : rows + r + 1] = line[:, cols - 1 :]
            if r == 0:
                rows_out[0, 1, part, :] = line.astype(b16)
            if r == rows - 1:
                rows_out[0, 0, part, :] = line.astype(b16)
        return carry

    lax.fori_loop(0, chunks, fill, 0)
    pl.semaphore_wait(barrier, 1 + sum(jnp.where(there, 1, 0) for _, _, there in places))

    def remote(source, target, send, recv, where):
        return pltpu.make_async_remote_copy(
            src_ref=source, dst_ref=target, send_sem=send, recv_sem=recv,
            device_id=where, device_id_type=mesh_ids,
        )

    def side(s, n):
        axis, place, _ = places[n]
        if n < 2:
            source, target = rows_out.at[s, n], rows_in.at[s, n]
        else:
            source, target = ends_t.at[s, pl.ds(0, 8)], beside.at[s, n - 2, pl.ds(0, 8)]
        return remote(source, target, side_send.at[s, n], side_recv.at[s, n], {axis: place})

    def chunk(s, i):
        part = pl.ds(pl.multiple_of(i * CHUNK, CHUNK), CHUNK)
        return remote(
            prop_16.at[s, part], other_16.at[s, part],
            chunk_send.at[s, i], chunk_recv.at[s, i], {"comp": 1 - me},
        )

    def sum_copy(s):
        return remote(sums.at[s], other_sums.at[s], sum_send.at[s], sum_recv.at[s], {"comp": 1 - me})

    def push(n):
        axis, place, _ = places[n]
        return remote(push_out, push_in.at[n], push_send.at[n], push_recv.at[n], {axis: place})

    lane = lax.broadcasted_iota(jnp.int32, (CHUNK, cols), 1)

    def step(s, carry):
        ends_t[s] = ends[...].T
        for n in range(4):
            @pl.when(places[n][2])
            def _(n=n):
                side(s, n).start()
        for n in range(4):
            @pl.when(places[n ^ 1][2])
            def _(n=n):
                side(s, n).wait_recv()
        ends[...] = beside[s, 0].T
        partial[: ends.shape[0], :cols] = beside[s, 1].T

        def body(i, totals):
            part = pl.ds(pl.multiple_of(i * CHUNK, CHUNK), CHUNK)
            tab = table[part, :]
            gx, gy, cos, sin, phase, ratio = (
                jnp.broadcast_to(tab[:, n : n + 1], (CHUNK, cols)) for n in range(6)
            )
            near_w = ends[part, :]
            near_e = partial[part, :cols]
            lines = [rows_in[s, 0, part, :].astype(f32)]
            lines += [state[part, r, :] for r in range(rows)]
            lines += [rows_in[s, 1, part, :].astype(f32)]
            out = []
            for r in range(rows):
                here = lines[r + 1]
                before = jnp.where(
                    lane == 0, near_w[:, rows + r : rows + r + 1], pltpu.roll(here, 1, 1)
                )
                after = jnp.where(
                    lane == cols - 1, near_e[:, r : r + 1], pltpu.roll(here, cols - 1, 1)
                )
                cx = gx + CURRENT_GAIN * currents[0, r : r + 1, :]
                cy = gy + CURRENT_GAIN * currents[1, r : r + 1, :]
                flux = jnp.abs(cx) * (here - jnp.where(cx > 0.0, before, after))
                flux = flux + jnp.abs(cy) * (here - jnp.where(cy > 0.0, lines[r], lines[r + 2]))
                moved = mask[r : r + 1, :] * (here - flux)
                prop[r, part, :] = moved
                prop_16[s, part, r * cols : (r + 1) * cols] = moved.astype(b16)
                growth = WIND_GAIN * jnp.maximum(
                    wind[0, r : r + 1, :] * cos + wind[1, r : r + 1, :] * sin - phase, 0.0
                )
                pushed = growth * moved
                for value in (moved, ratio * moved, pushed * cos, pushed * sin):
                    out.append(value.reshape(CHUNK // 8, 8, cols).sum(axis=0))
            chunk(s, i).start()
            return tuple(t + o for t, o in zip(totals, out))

        zero = jnp.zeros((8, cols), f32)
        totals = lax.fori_loop(0, chunks, body, (zero,) * (4 * rows))
        for r in range(rows):
            for n in range(4):
                at = n * rows + r
                sums[s, at : at + 1, :] = totals[4 * r + n].sum(axis=0, keepdims=True)
        sum_copy(s).start()
        own = pl.multiple_of(me * comps, comps)
        partial[...] = dot_0(first[pl.ds(own, comps), :], prop_16[s])
        sum_copy(s).wait_recv()
        total = sums[s] + other_sums[s]
        pushes[...] += total[2 * rows :, :]

        @pl.when(s == STEPS - 1)
        def _():
            push_out[...] = pushes[...]
            for n in range(2):
                @pl.when(places[n][2])
                def _(n=n):
                    push(n).start()

        scale_up = 2.0 * comps
        floor = jnp.maximum(total[:rows, :], 1.0)
        spread_ratio = total[rows : 2 * rows, :] / floor
        squared = DECAY_GAIN * spread_ratio * spread_ratio
        gain = scale_up / floor
        back = NONLINEAR_GAIN * (floor / scale_up)

        far_start = pl.multiple_of((1 - me) * comps, comps)
        group = chunks // PIECES
        span = group * CHUNK
        for g in range(PIECES):
            for i in range(g * group, (g + 1) * group):
                chunk(s, i).wait_recv()
            at = pl.multiple_of(far_start + g * span, span)
            pre = dot_0(first[pl.ds(at, span), :], other_16[s, g * span : (g + 1) * span, :])
            pre = pre + partial[...]
            if g < PIECES - 1:
                partial[...] = pre
        pre = pre * jnp.concatenate([gain[r : r + 1, :] for r in range(rows)], axis=1)
        hidden[...] = (pre / (1.0 + jnp.exp(-pre))).astype(b16)
        transfer[...] = dot_0(second[...], hidden[...]).astype(b16)
        later = jnp.minimum(s + 1, STEPS - 1)

        for n in range(4):
            @pl.when(places[n][2])
            def _(n=n):
                side(s, n).wait_send()

        def update(i, carry):
            part = pl.ds(pl.multiple_of(i * CHUNK, CHUNK), CHUNK)
            tab = table[part, :]
            cos, sin, phase, ratio = (
                jnp.broadcast_to(tab[:, n : n + 1], (CHUNK, cols)) for n in range(2, 6)
            )
            for r in range(rows):
                growth = WIND_GAIN * jnp.maximum(
                    wind[0, r : r + 1, :] * cos + wind[1, r : r + 1, :] * sin - phase, 0.0
                )
                fresh = prop[r, part, :] * jnp.exp(growth - ratio * squared[r : r + 1, :])
                moved = transfer[part, r * cols : (r + 1) * cols].astype(f32)
                fresh = fresh + back[r : r + 1, :] * moved
                state[part, r, :] = fresh
                ends[part, r : r + 1] = fresh[:, :1]
                ends[part, rows + r : rows + r + 1] = fresh[:, cols - 1 :]
                if r == 0:
                    rows_out[later, 1, part, :] = fresh.astype(b16)
                if r == rows - 1:
                    rows_out[later, 0, part, :] = fresh.astype(b16)
            return carry

        lax.fori_loop(0, chunks, update, 0)

        def leave(i, carry):
            chunk(s, i).wait_send()
            return carry

        lax.fori_loop(0, chunks, leave, 0)
        sum_copy(s).wait_send()
        return carry

    lax.fori_loop(0, STEPS, step, 0)
    for n in range(2):
        @pl.when(places[n][2])
        def _(n=n):
            push(n).wait_send()

        @pl.when(places[n ^ 1][2])
        def _(n=n):
            push(n).wait_recv()
    push_from[...] = push_in[...]


def steps_call(first, state, second, table, currents, wind, mask):
    comps, rows, cols = state.shape
    units = first.shape[1]
    cells = rows * cols
    f32, b16 = jnp.float32, jnp.bfloat16
    wide = -(-comps // 128) * 128
    shape = jax.ShapeDtypeStruct
    dma = pltpu.SemaphoreType.DMA
    chunks = comps // CHUNK
    return pl.pallas_call(
        step_kernel,
        out_shape=(
            shape((comps, rows, cols), f32),
            shape((2 * rows, cols), f32),
            shape((2, 2 * rows, cols), f32),
        ),
        in_specs=[pl.BlockSpec(memory_space=pltpu.VMEM)] * 7,
        out_specs=(pl.BlockSpec(memory_space=pltpu.VMEM),) * 3,
        scratch_shapes=[
            pltpu.VMEM((rows, comps, cols), f32),
            pltpu.VMEM((STEPS, comps, cells), b16),
            pltpu.VMEM((STEPS, comps, cells), b16),
            pltpu.VMEM((wide, 128), f32),
            pltpu.VMEM((STEPS, 128, wide), f32),
            pltpu.VMEM((STEPS, 2, 128, wide), f32),
            pltpu.VMEM((STEPS, 2, comps, cols), b16),
            pltpu.VMEM((STEPS, 2, comps, cols), b16),
            pltpu.VMEM((STEPS, 4 * rows, cols), f32),
            pltpu.VMEM((STEPS, 4 * rows, cols), f32),
            pltpu.VMEM((2 * rows, cols), f32),
            pltpu.VMEM((2, 2 * rows, cols), f32),
            pltpu.VMEM((units, cells), b16),
            pltpu.VMEM((comps, cells), b16),
            pltpu.VMEM((units, cells), f32),
            dma((STEPS, 4)),
            dma((STEPS, 4)),
            dma((STEPS, chunks)),
            dma((STEPS, chunks)),
            dma((STEPS,)),
            dma((STEPS,)),
            dma((2,)),
            dma((2,)),
        ],
        compiler_params=pltpu.CompilerParams(
            vmem_limit_bytes=VMEM_LIMIT, collective_id=0, has_side_effects=True
        ),
        cost_estimate=pl.CostEstimate(
            flops=12 * comps * units * cells, bytes_accessed=24 * comps * cells, transcendentals=0
        ),
    )(first, state, second, table, currents, wind, mask)


def ocean_kernel(
    state, south, north, west, east, low, high, ends, ends_t, rows_in, beside, send, recv
):
    count_all, rows, _ = state.shape
    places = []
    for axis in ("gy", "gx"):
        at, count = lax.axis_index(axis), lax.axis_size(axis)
        places.append((axis, lax.rem(at + 1, count), at < count - 1))
        places.append((axis, lax.rem(at + count - 1, count), at > 0))
    rows_in[...] = jnp.zeros_like(rows_in)
    beside[...] = jnp.zeros_like(beside)
    mesh_ids = pl.DeviceIdType.MESH
    barrier = pltpu.get_barrier_semaphore()
    for axis, place, there in places:
        @pl.when(there)
        def _(axis=axis, place=place):
            pl.semaphore_signal(barrier, inc=1, device_id={axis: place}, device_id_type=mesh_ids)
    ends[...] = jnp.zeros_like(ends)
    low[...] = state[:, 0, :]
    high[...] = state[:, rows - 1, :]
    for r in range(rows):
        line = state[:, r, :]
        ends[:count_all, r : r + 1] = line[:, :1]
        ends[:count_all, rows + r : rows + r + 1] = line[:, -1:]
    ends_t[...] = ends[...].T
    pl.semaphore_wait(barrier, sum(jnp.where(there, 1, 0) for _, _, there in places))

    def side(n):
        axis, place, _ = places[n]
        if n < 2:
            source, target = (high, low)[n], rows_in.at[n]
        else:
            source, target = ends_t.at[pl.ds(0, 8)], beside.at[n - 2, pl.ds(0, 8)]
        return pltpu.make_async_remote_copy(
            src_ref=source, dst_ref=target, send_sem=send.at[n], recv_sem=recv.at[n],
            device_id={axis: place}, device_id_type=mesh_ids,
        )

    for n in range(4):
        @pl.when(places[n][2])
        def _(n=n):
            side(n).start()
    for n in range(4):
        @pl.when(places[n ^ 1][2])
        def _(n=n):
            side(n).wait_recv()

        @pl.when(places[n][2])
        def _(n=n):
            side(n).wait_send()
    south[...] = rows_in[0]
    north[...] = rows_in[1]
    west[...] = beside[0].T[:count_all, rows : 2 * rows]
    east[...] = beside[1].T[:count_all, :rows]


def ocean_call(state):
    count_all, rows, cols = state.shape
    f32 = jnp.float32
    wide = -(-count_all // 128) * 128
    shape = jax.ShapeDtypeStruct
    return pl.pallas_call(
        ocean_kernel,
        out_shape=(shape((count_all, cols), f32),) * 2 + (shape((count_all, rows), f32),) * 2,
        in_specs=[pl.BlockSpec(memory_space=pltpu.VMEM)],
        out_specs=(pl.BlockSpec(memory_space=pltpu.VMEM),) * 4,
        scratch_shapes=[
            pltpu.VMEM((count_all, cols), f32),
            pltpu.VMEM((count_all, cols), f32),
            pltpu.VMEM((wide, 128), f32),
            pltpu.VMEM((128, wide), f32),
            pltpu.VMEM((2, count_all, cols), f32),
            pltpu.VMEM((2, 128, wide), f32),
            pltpu.SemaphoreType.DMA((4,)),
            pltpu.SemaphoreType.DMA((4,)),
        ],
        compiler_params=pltpu.CompilerParams(collective_id=1, has_side_effects=True),
        cost_estimate=pl.CostEstimate(flops=100000, bytes_accessed=400000, transcendentals=0),
    )(state)


def ocean_update(padded, stress, mask_f):

    def middle(field):
        return field[..., 1:-1, 1:-1]

    def eastern(field):
        return field[..., 1:-1, 2:]

    def western(field):
        return field[..., 1:-1, :-2]

    def northern(field):
        return field[..., 2:, 1:-1]

    def southern(field):
        return field[..., :-2, 1:-1]

    def spread(field):
        return (
            eastern(field)
            + western(field)
            + northern(field)
            + southern(field)
            - 4.0 * middle(field)
        )

    def column(field):
        upper_level = jnp.concatenate([field[:1], field[:-1]], axis=0)
        lower_level = jnp.concatenate([field[1:], field[-1:]], axis=0)
        return upper_level + lower_level - 2.0 * field

    density = -THERMAL * padded[2] + HALINE * padded[3]
    pressure = jnp.cumsum(density, axis=0) - 0.5 * density
    speed_u = middle(padded[0])
    speed_v = middle(padded[1])

    def carry_term(field):
        return speed_u * 0.5 * (eastern(field) - western(field)) + speed_v * 0.5 * (
            northern(field) - southern(field)
        )

    surface = (jnp.arange(padded.shape[1]) == 0).astype(jnp.float32)[:, None, None]
    tend_u = (
        CORIOLIS * speed_v
        - PRESSURE_GAIN * 0.5 * (eastern(pressure) - western(pressure))
        + LATERAL_MIX * spread(padded[0])
        + VERTICAL_MIX * column(speed_u)
        + STRESS_GAIN * surface * stress[0]
    )
    tend_v = (
        -CORIOLIS * speed_u
        - PRESSURE_GAIN * 0.5 * (northern(pressure) - southern(pressure))
        + LATERAL_MIX * spread(padded[1])
        + VERTICAL_MIX * column(speed_v)
        + STRESS_GAIN * surface * stress[1]
    )
    tend_t = (
        -ADVECTION * carry_term(padded[2])
        + LATERAL_MIX * spread(padded[2])
        + VERTICAL_MIX * column(middle(padded[2]))
    )
    tend_s = (
        -ADVECTION * carry_term(padded[3])
        + LATERAL_MIX * spread(padded[3])
        + VERTICAL_MIX * column(middle(padded[3]))
    )
    return middle(padded) + mask_f * jnp.stack([tend_u, tend_v, tend_t, tend_s])


def regrid(field, below, above, blocks, row_table):
    rows = field.shape[1]
    padded = jnp.concatenate([below, field, above], axis=1)
    first_row = lax.axis_index("gy") * rows
    offset = row_table[:, :, 0] - first_row - jnp.arange(rows)[:, None]
    offset = offset[None, :, :, None]
    selected = jnp.where(
        offset < 0,
        padded[:, :rows, None, :],
        jnp.where(offset == 0, padded[:, 1:-1, None, :], padded[:, 2:, None, :]),
    )
    return jnp.einsum("rbds,krbs->krd", blocks, selected, precision=lax.Precision.HIGHEST)


def local(
    spectra,
    wind_field,
    sea_mask,
    first_layer,
    second_layer,
    ocean_state,
    current_blocks,
    current_rows,
    stress_blocks,
    stress_rows,
):
    f32 = jnp.float32
    mask_f = sea_mask.astype(f32)
    rows, cols = sea_mask.shape
    half_freqs, directions = spectra.shape[:2]
    comps = half_freqs * directions
    total = 2 * comps
    me = lax.axis_index("comp")
    table = lax.dynamic_slice_in_dim(
        jnp.asarray(tables(2 * half_freqs, directions)), me * comps, comps, 0
    )
    levels = ocean_state.shape[1]
    south, north, west, east = ocean_call(ocean_state.reshape(4 * levels, rows, cols))
    ocean_south = south.reshape(4, levels, 1, cols)
    ocean_north = north.reshape(4, levels, 1, cols)
    ocean_west = west.reshape(4, levels, rows, 1)
    ocean_east = east.reshape(4, levels, rows, 1)
    currents = regrid(
        ocean_state[:2, 0], ocean_south[:2, 0], ocean_north[:2, 0], current_blocks, current_rows
    )
    second_own = lax.dynamic_slice_in_dim(second_layer, me * comps, comps, 1)
    state, pushes, push_from = steps_call(
        first_layer,
        spectra.reshape(comps, rows, cols),
        second_own,
        table,
        currents,
        wind_field,
        mask_f,
    )
    whole = jnp.concatenate([pushes[None], push_from]) / (STEPS * total)
    whole = whole.reshape(3, 2, rows, cols)
    stress_ocean = regrid(
        whole[0], whole[1, :, -1:], whole[2, :, :1], stress_blocks, stress_rows
    )
    corner = jnp.zeros(ocean_west.shape[:2] + (1, 1), f32)
    padded = jnp.concatenate(
        [
            jnp.concatenate([corner, ocean_south, corner], axis=3),
            jnp.concatenate([ocean_west, ocean_state, ocean_east], axis=3),
            jnp.concatenate([corner, ocean_north, corner], axis=3),
        ],
        axis=2,
    )
    return (state.reshape(spectra.shape), ocean_update(padded, stress_ocean, mask_f))


def solution(mesh):
    placed = (
        P("comp", None, "gy", "gx"),
        P(None, "gy", "gx"),
        P("gy", "gx"),
        P(),
        P(),
        P(None, None, "gy", "gx"),
        P("gy", None, "gx", None),
        P("gy", None, "gx"),
        P("gy", None, "gx", None),
        P("gy", None, "gx"),
    )
    return jax.shard_map(
        local,
        mesh=mesh,
        in_specs=placed,
        out_specs=(P("comp", None, "gy", "gx"), P(None, None, "gy", "gx")),
        check_vma=False,
    )
```

```python
import numpy as np

import jax
import jax.numpy as jnp
from jax import lax
from jax.experimental import pallas as pl
from jax.experimental.pallas import tpu as pltpu
from jax.sharding import PartitionSpec as P

STEPS = 2


CURRENT_GAIN = 0.08
WIND_GAIN = 0.06
DECAY_GAIN = 0.03
NONLINEAR_GAIN = 0.3
THERMAL = 0.2
HALINE = 0.8
CORIOLIS = 0.1
PRESSURE_GAIN = 0.2
LATERAL_MIX = 0.1
VERTICAL_MIX = 0.2
ADVECTION = 0.3
STRESS_GAIN = 150.0


def tables(total, directions):
    index = np.arange(total, dtype=np.float64)
    group = 0.4 * np.exp(-3.0 * index / (total - 1))
    ratio = np.exp(2.0 * index / (total - 1) - 1.0)
    angles = 2.0 * np.pi * np.arange(directions) / directions
    cosines, sines = np.cos(angles), np.sin(angles)
    full = np.zeros((total, directions, 8))
    full[..., 0] = group[:, None] * cosines
    full[..., 1] = group[:, None] * sines
    full[..., 2] = cosines
    full[..., 3] = sines
    full[..., 4] = 4.0 * group[:, None]
    full[..., 5] = ratio[:, None]
    return full.reshape(total * directions, 8).astype(np.float32)


VMEM_LIMIT = 56 * 1024 * 1024
CHUNK = 48
PIECES = 3


def dot_0(left, right):
    return lax.dot_general(
        left, right, (((0,), (0,)), ((), ())), preferred_element_type=jnp.float32
    )


def step_kernel(
    first, spectra, second, table, currents, wind, mask,
    state, pushes, push_from,
    prop, prop_16, other_16, ends, ends_t, beside, rows_out, rows_in, sums, other_sums,
    push_out, push_in, hidden, transfer, partial, side_send, side_recv, chunk_send, chunk_recv,
    sum_send, sum_recv, push_send, push_recv,
):
    comps, rows, cols = state.shape
    f32, b16 = jnp.float32, jnp.bfloat16
    chunks = comps // CHUNK
    me = lax.axis_index("comp")
    places = []
    for axis in ("gy", "gx"):
        at, count = lax.axis_index(axis), lax.axis_size(axis)
        places.append((axis, lax.rem(at + 1, count), at < count - 1))
        places.append((axis, lax.rem(at + count - 1, count), at > 0))
    beside[...] = jnp.zeros_like(beside)
    rows_in[...] = jnp.zeros_like(rows_in)
    push_in[...] = jnp.zeros_like(push_in)
    pushes[...] = jnp.zeros_like(pushes)
    ends[...] = jnp.zeros_like(ends)

    mesh_ids = pl.DeviceIdType.MESH
    barrier = pltpu.get_barrier_semaphore()
    for axis, place, there in places:
        @pl.when(there)
        def _(axis=axis, place=place):
            pl.semaphore_signal(barrier, inc=1, device_id={axis: place}, device_id_type=mesh_ids)
    pl.semaphore_signal(barrier, inc=1, device_id={"comp": 1 - me}, device_id_type=mesh_ids)

    def fill(i, carry):
        part = pl.ds(pl.multiple_of(i * CHUNK, CHUNK), CHUNK)
        for r in range(rows):
            line = spectra[part, r, :]
            state[part, r, :] = line
            ends[part, r : r + 1] = line[:, :1]
            ends[part, rows + r : rows + r + 1] = line[:, cols - 1 :]
            if r == 0:
                rows_out[0, 1, part, :] = line.astype(b16)
            if r == rows - 1:
                rows_out[0, 0, part, :] = line.astype(b16)
        return carry

    lax.fori_loop(0, chunks, fill, 0)
    pl.semaphore_wait(barrier, 1 + sum(jnp.where(there, 1, 0) for _, _, there in places))

    def remote(source, target, send, recv, where):
        return pltpu.make_async_remote_copy(
            src_ref=source, dst_ref=target, send_sem=send, recv_sem=recv,
            device_id=where, device_id_type=mesh_ids,
        )

    def side(s, n):
        axis, place, _ = places[n]
        if n < 2:
            source, target = rows_out.at[s, n], rows_in.at[s, n]
        else:
            source, target = ends_t.at[s, pl.ds(0, 8)], beside.at[s, n - 2, pl.ds(0, 8)]
        return remote(source, target, side_send.at[s, n], side_recv.at[s, n], {axis: place})

    def chunk(s, i):
        part = pl.ds(pl.multiple_of(i * CHUNK, CHUNK), CHUNK)
        return remote(
            prop_16.at[s, part], other_16.at[s, part],
            chunk_send.at[s, i], chunk_recv.at[s, i], {"comp": 1 - me},
        )

    def sum_copy(s):
        return remote(sums.at[s], other_sums.at[s], sum_send.at[s], sum_recv.at[s], {"comp": 1 - me})

    def push(n):
        axis, place, _ = places[n]
        return remote(push_out, push_in.at[n], push_send.at[n], push_recv.at[n], {axis: place})

    lane = lax.broadcasted_iota(jnp.int32, (CHUNK, cols), 1)

    def step(s, carry):
        ends_t[s] = ends[...].T
        for n in range(4):
            @pl.when(places[n][2])
            def _(n=n):
                side(s, n).start()
        for n in range(4):
            @pl.when(places[n ^ 1][2])
            def _(n=n):
                side(s, n).wait_recv()
        ends[...] = beside[s, 0].T
        partial[: ends.shape[0], :cols] = beside[s, 1].T

        def body(i, totals):
            part = pl.ds(pl.multiple_of(i * CHUNK, CHUNK), CHUNK)
            tab = table[pl.ds(pl.multiple_of(me * comps + i * CHUNK, CHUNK), CHUNK), :]
            gx, gy, cos, sin, phase, ratio = (
                jnp.broadcast_to(tab[:, n : n + 1], (CHUNK, cols)) for n in range(6)
            )
            near_w = ends[part, :]
            near_e = partial[part, :cols]
            lines = [rows_in[s, 0, part, :].astype(f32)]
            lines += [state[part, r, :] for r in range(rows)]
            lines += [rows_in[s, 1, part, :].astype(f32)]
            out = []
            for r in range(rows):
                here = lines[r + 1]
                before = jnp.where(
                    lane == 0, near_w[:, rows + r : rows + r + 1], pltpu.roll(here, 1, 1)
                )
                after = jnp.where(
                    lane == cols - 1, near_e[:, r : r + 1], pltpu.roll(here, cols - 1, 1)
                )
                cx = gx + CURRENT_GAIN * currents[0, r : r + 1, :]
                cy = gy + CURRENT_GAIN * currents[1, r : r + 1, :]
                flux = jnp.abs(cx) * (here - jnp.where(cx > 0.0, before, after))
                flux = flux + jnp.abs(cy) * (here - jnp.where(cy > 0.0, lines[r], lines[r + 2]))
                moved = mask[r : r + 1, :].astype(f32) * (here - flux)
                prop[r, part, :] = moved
                prop_16[s, part, r * cols : (r + 1) * cols] = moved.astype(b16)
                growth = WIND_GAIN * jnp.maximum(
                    wind[0, r : r + 1, :] * cos + wind[1, r : r + 1, :] * sin - phase, 0.0
                )
                pushed = growth * moved
                for value in (moved, ratio * moved, pushed * cos, pushed * sin):
                    out.append(value.reshape(CHUNK // 8, 8, cols).sum(axis=0))
            chunk(s, i).start()
            return tuple(t + o for t, o in zip(totals, out))

        zero = jnp.zeros((8, cols), f32)
        totals = lax.fori_loop(0, chunks, body, (zero,) * (4 * rows))
        for r in range(rows):
            for n in range(4):
                at = n * rows + r
                sums[s, at : at + 1, :] = totals[4 * r + n].sum(axis=0, keepdims=True)
        sum_copy(s).start()
        own = pl.multiple_of(me * comps, comps)
        partial[...] = dot_0(first[pl.ds(own, comps), :], prop_16[s])
        sum_copy(s).wait_recv()
        total = sums[s] + other_sums[s]
        pushes[...] += total[2 * rows :, :]

        @pl.when(s == STEPS - 1)
        def _():
            push_out[...] = pushes[...]
            for n in range(2):
                @pl.when(places[n][2])
                def _(n=n):
                    push(n).start()

        scale_up = 2.0 * comps
        floor = jnp.maximum(total[:rows, :], 1.0)
        spread_ratio = total[rows : 2 * rows, :] / floor
        squared = DECAY_GAIN * spread_ratio * spread_ratio
        gain = scale_up / floor
        back = NONLINEAR_GAIN * (floor / scale_up)

        far_start = pl.multiple_of((1 - me) * comps, comps)
        group = chunks // PIECES
        span = group * CHUNK
        for g in range(PIECES):
            for i in range(g * group, (g + 1) * group):
                chunk(s, i).wait_recv()
            at = pl.multiple_of(far_start + g * span, span)
            pre = dot_0(first[pl.ds(at, span), :], other_16[s, g * span : (g + 1) * span, :])
            pre = pre + partial[...]
            if g < PIECES - 1:
                partial[...] = pre
        pre = pre * jnp.concatenate([gain[r : r + 1, :] for r in range(rows)], axis=1)
        hidden[...] = (pre / (1.0 + jnp.exp(-pre))).astype(b16)
        transfer[...] = dot_0(second[...], hidden[...]).astype(b16)
        later = jnp.minimum(s + 1, STEPS - 1)

        for n in range(4):
            @pl.when(places[n][2])
            def _(n=n):
                side(s, n).wait_send()

        def update(i, carry):
            part = pl.ds(pl.multiple_of(i * CHUNK, CHUNK), CHUNK)
            tab = table[pl.ds(pl.multiple_of(me * comps + i * CHUNK, CHUNK), CHUNK), :]
            cos, sin, phase, ratio = (
                jnp.broadcast_to(tab[:, n : n + 1], (CHUNK, cols)) for n in range(2, 6)
            )
            for r in range(rows):
                growth = WIND_GAIN * jnp.maximum(
                    wind[0, r : r + 1, :] * cos + wind[1, r : r + 1, :] * sin - phase, 0.0
                )
                fresh = prop[r, part, :] * jnp.exp(growth - ratio * squared[r : r + 1, :])
                moved = transfer[part, r * cols : (r + 1) * cols].astype(f32)
                fresh = fresh + back[r : r + 1, :] * moved
                state[part, r, :] = fresh
                ends[part, r : r + 1] = fresh[:, :1]
                ends[part, rows + r : rows + r + 1] = fresh[:, cols - 1 :]
                if r == 0:
                    rows_out[later, 1, part, :] = fresh.astype(b16)
                if r == rows - 1:
                    rows_out[later, 0, part, :] = fresh.astype(b16)
            return carry

        lax.fori_loop(0, chunks, update, 0)

        def leave(i, carry):
            chunk(s, i).wait_send()
            return carry

        lax.fori_loop(0, chunks, leave, 0)
        sum_copy(s).wait_send()
        return carry

    lax.fori_loop(0, STEPS, step, 0)
    for n in range(2):
        @pl.when(places[n][2])
        def _(n=n):
            push(n).wait_send()

        @pl.when(places[n ^ 1][2])
        def _(n=n):
            push(n).wait_recv()
    push_from[...] = push_in[...]


def steps_call(first, state, second, table, currents, wind, mask):
    comps, rows, cols = state.shape
    units = first.shape[1]
    cells = rows * cols
    f32, b16 = jnp.float32, jnp.bfloat16
    wide = -(-comps // 128) * 128
    shape = jax.ShapeDtypeStruct
    dma = pltpu.SemaphoreType.DMA
    chunks = comps // CHUNK
    return pl.pallas_call(
        step_kernel,
        out_shape=(
            shape((comps, rows, cols), f32),
            shape((2 * rows, cols), f32),
            shape((2, 2 * rows, cols), f32),
        ),
        in_specs=[pl.BlockSpec(memory_space=pltpu.VMEM)] * 7,
        out_specs=(pl.BlockSpec(memory_space=pltpu.VMEM),) * 3,
        scratch_shapes=[
            pltpu.VMEM((rows, comps, cols), f32),
            pltpu.VMEM((STEPS, comps, cells), b16),
            pltpu.VMEM((STEPS, comps, cells), b16),
            pltpu.VMEM((wide, 128), f32),
            pltpu.VMEM((STEPS, 128, wide), f32),
            pltpu.VMEM((STEPS, 2, 128, wide), f32),
            pltpu.VMEM((STEPS, 2, comps, cols), b16),
            pltpu.VMEM((STEPS, 2, comps, cols), b16),
            pltpu.VMEM((STEPS, 4 * rows, cols), f32),
            pltpu.VMEM((STEPS, 4 * rows, cols), f32),
            pltpu.VMEM((2 * rows, cols), f32),
            pltpu.VMEM((2, 2 * rows, cols), f32),
            pltpu.VMEM((units, cells), b16),
            pltpu.VMEM((comps, cells), b16),
            pltpu.VMEM((units, cells), f32),
            dma((STEPS, 4)),
            dma((STEPS, 4)),
            dma((STEPS, chunks)),
            dma((STEPS, chunks)),
            dma((STEPS,)),
            dma((STEPS,)),
            dma((2,)),
            dma((2,)),
        ],
        compiler_params=pltpu.CompilerParams(
            vmem_limit_bytes=VMEM_LIMIT, collective_id=0, has_side_effects=True
        ),
        cost_estimate=pl.CostEstimate(
            flops=12 * comps * units * cells, bytes_accessed=24 * comps * cells, transcendentals=0
        ),
    )(first, state, second, table, currents, wind, mask)


def ocean_kernel(
    state, south, north, west, east, low, high, ends, ends_t, rows_in, beside, send, recv
):
    count_all, rows, _ = state.shape
    places = []
    for axis in ("gy", "gx"):
        at, count = lax.axis_index(axis), lax.axis_size(axis)
        places.append((axis, lax.rem(at + 1, count), at < count - 1))
        places.append((axis, lax.rem(at + count - 1, count), at > 0))
    rows_in[...] = jnp.zeros_like(rows_in)
    beside[...] = jnp.zeros_like(beside)
    mesh_ids = pl.DeviceIdType.MESH
    barrier = pltpu.get_barrier_semaphore()
    for axis, place, there in places:
        @pl.when(there)
        def _(axis=axis, place=place):
            pl.semaphore_signal(barrier, inc=1, device_id={axis: place}, device_id_type=mesh_ids)
    ends[...] = jnp.zeros_like(ends)
    low[...] = state[:, 0, :]
    high[...] = state[:, rows - 1, :]
    for r in range(rows):
        line = state[:, r, :]
        ends[:count_all, r : r + 1] = line[:, :1]
        ends[:count_all, rows + r : rows + r + 1] = line[:, -1:]
    ends_t[...] = ends[...].T
    pl.semaphore_wait(barrier, sum(jnp.where(there, 1, 0) for _, _, there in places))

    def side(n):
        axis, place, _ = places[n]
        if n < 2:
            source, target = (high, low)[n], rows_in.at[n]
        else:
            source, target = ends_t.at[pl.ds(0, 8)], beside.at[n - 2, pl.ds(0, 8)]
        return pltpu.make_async_remote_copy(
            src_ref=source, dst_ref=target, send_sem=send.at[n], recv_sem=recv.at[n],
            device_id={axis: place}, device_id_type=mesh_ids,
        )

    for n in range(4):
        @pl.when(places[n][2])
        def _(n=n):
            side(n).start()
    for n in range(4):
        @pl.when(places[n ^ 1][2])
        def _(n=n):
            side(n).wait_recv()

        @pl.when(places[n][2])
        def _(n=n):
            side(n).wait_send()
    south[...] = rows_in[0]
    north[...] = rows_in[1]
    west[...] = beside[0].T[:count_all, rows : 2 * rows]
    east[...] = beside[1].T[:count_all, :rows]


def ocean_call(state):
    count_all, rows, cols = state.shape
    f32 = jnp.float32
    wide = -(-count_all // 128) * 128
    shape = jax.ShapeDtypeStruct
    return pl.pallas_call(
        ocean_kernel,
        out_shape=(shape((count_all, cols), f32),) * 2 + (shape((count_all, rows), f32),) * 2,
        in_specs=[pl.BlockSpec(memory_space=pltpu.VMEM)],
        out_specs=(pl.BlockSpec(memory_space=pltpu.VMEM),) * 4,
        scratch_shapes=[
            pltpu.VMEM((count_all, cols), f32),
            pltpu.VMEM((count_all, cols), f32),
            pltpu.VMEM((wide, 128), f32),
            pltpu.VMEM((128, wide), f32),
            pltpu.VMEM((2, count_all, cols), f32),
            pltpu.VMEM((2, 128, wide), f32),
            pltpu.SemaphoreType.DMA((4,)),
            pltpu.SemaphoreType.DMA((4,)),
        ],
        compiler_params=pltpu.CompilerParams(collective_id=1, has_side_effects=True),
        cost_estimate=pl.CostEstimate(flops=100000, bytes_accessed=400000, transcendentals=0),
    )(state)


def ocean_update(padded, stress, mask_f):

    def middle(field):
        return field[..., 1:-1, 1:-1]

    def eastern(field):
        return field[..., 1:-1, 2:]

    def western(field):
        return field[..., 1:-1, :-2]

    def northern(field):
        return field[..., 2:, 1:-1]

    def southern(field):
        return field[..., :-2, 1:-1]

    def spread(field):
        return (
            eastern(field)
            + western(field)
            + northern(field)
            + southern(field)
            - 4.0 * middle(field)
        )

    def column(field):
        upper_level = jnp.concatenate([field[:1], field[:-1]], axis=0)
        lower_level = jnp.concatenate([field[1:], field[-1:]], axis=0)
        return upper_level + lower_level - 2.0 * field

    density = -THERMAL * padded[2] + HALINE * padded[3]
    pressure = jnp.cumsum(density, axis=0) - 0.5 * density
    speed_u = middle(padded[0])
    speed_v = middle(padded[1])

    def carry_term(field):
        return speed_u * 0.5 * (eastern(field) - western(field)) + speed_v * 0.5 * (
            northern(field) - southern(field)
        )

    surface = (jnp.arange(padded.shape[1]) == 0).astype(jnp.float32)[:, None, None]
    tend_u = (
        CORIOLIS * speed_v
        - PRESSURE_GAIN * 0.5 * (eastern(pressure) - western(pressure))
        + LATERAL_MIX * spread(padded[0])
        + VERTICAL_MIX * column(speed_u)
        + STRESS_GAIN * surface * stress[0]
    )
    tend_v = (
        -CORIOLIS * speed_u
        - PRESSURE_GAIN * 0.5 * (northern(pressure) - southern(pressure))
        + LATERAL_MIX * spread(padded[1])
        + VERTICAL_MIX * column(speed_v)
        + STRESS_GAIN * surface * stress[1]
    )
    tend_t = (
        -ADVECTION * carry_term(padded[2])
        + LATERAL_MIX * spread(padded[2])
        + VERTICAL_MIX * column(middle(padded[2]))
    )
    tend_s = (
        -ADVECTION * carry_term(padded[3])
        + LATERAL_MIX * spread(padded[3])
        + VERTICAL_MIX * column(middle(padded[3]))
    )
    return middle(padded) + mask_f * jnp.stack([tend_u, tend_v, tend_t, tend_s])


def regrid(field, below, above, blocks, row_table):
    rows = field.shape[1]
    padded = jnp.concatenate([below, field, above], axis=1)
    first_row = lax.axis_index("gy") * rows
    offset = row_table[:, :, 0] - first_row - jnp.arange(rows)[:, None]
    offset = offset[None, :, :, None]
    selected = jnp.where(
        offset < 0,
        padded[:, :rows, None, :],
        jnp.where(offset == 0, padded[:, 1:-1, None, :], padded[:, 2:, None, :]),
    )
    return jnp.einsum("rbds,krbs->krd", blocks, selected, precision=lax.Precision.HIGHEST)


def local(
    spectra,
    wind_field,
    sea_mask,
    first_layer,
    second_layer,
    ocean_state,
    current_blocks,
    current_rows,
    stress_blocks,
    stress_rows,
):
    f32 = jnp.float32
    mask_f = sea_mask.astype(f32)
    rows, cols = sea_mask.shape
    half_freqs, directions = spectra.shape[:2]
    comps = half_freqs * directions
    total = 2 * comps
    me = lax.axis_index("comp")
    table = jnp.asarray(tables(2 * half_freqs, directions))
    levels = ocean_state.shape[1]
    south, north, west, east = ocean_call(ocean_state.reshape(4 * levels, rows, cols))
    ocean_south = south.reshape(4, levels, 1, cols)
    ocean_north = north.reshape(4, levels, 1, cols)
    ocean_west = west.reshape(4, levels, rows, 1)
    ocean_east = east.reshape(4, levels, rows, 1)
    currents = regrid(
        ocean_state[:2, 0], ocean_south[:2, 0], ocean_north[:2, 0], current_blocks, current_rows
    )
    second_own = lax.dynamic_slice_in_dim(second_layer, me * comps, comps, 1)
    state, pushes, push_from = steps_call(
        first_layer,
        spectra.reshape(comps, rows, cols),
        second_own,
        table,
        currents,
        wind_field,
        sea_mask,
    )
    whole = jnp.concatenate([pushes[None], push_from]) / (STEPS * total)
    whole = whole.reshape(3, 2, rows, cols)
    stress_ocean = regrid(
        whole[0], whole[1, :, -1:], whole[2, :, :1], stress_blocks, stress_rows
    )
    corner = jnp.zeros(ocean_west.shape[:2] + (1, 1), f32)
    padded = jnp.concatenate(
        [
            jnp.concatenate([corner, ocean_south, corner], axis=3),
            jnp.concatenate([ocean_west, ocean_state, ocean_east], axis=3),
            jnp.concatenate([corner, ocean_north, corner], axis=3),
        ],
        axis=2,
    )
    return (state.reshape(spectra.shape), ocean_update(padded, stress_ocean, mask_f))


def solution(mesh):
    placed = (
        P("comp", None, "gy", "gx"),
        P(None, "gy", "gx"),
        P("gy", "gx"),
        P(),
        P(),
        P(None, None, "gy", "gx"),
        P("gy", None, "gx", None),
        P("gy", None, "gx"),
        P("gy", None, "gx", None),
        P("gy", None, "gx"),
    )
    return jax.shard_map(
        local,
        mesh=mesh,
        in_specs=placed,
        out_specs=(P("comp", None, "gy", "gx"), P(None, None, "gy", "gx")),
        check_vma=False,
    )
```
